32 devices in a mesh: node: 8 (over z, x), local: 4 (over y, core).
Axes of the slice: x: 2, y: 2, z: 4, core: 2. Of those that a mesh axis runs over, the one named last changes fastest.
Arguments:
- tokens: bfloat16 [512, 7168], P('node'), may hold values from -6 to 6
- router_weight: bfloat16 [7168, 32], replicated, may hold values from -0.125 to 0.125
- expert_ids: int32 [512, 8], P('node'), may hold values from 0 to 31, as said below
- gate_weight: bfloat16 [32, 7168, 2048], P('node', None, 'local'), may hold values from -0.0625 to 0.0625
- up_weight: bfloat16 [32, 7168, 2048], P('node', None, 'local'), may hold values from -0.0625 to 0.0625
- down_weight: bfloat16 [32, 2048, 7168], P('node', 'local'), may hold values from -0.125 to 0.125
Outputs:
- combined: bfloat16 [512, 7168], P('node', 'local')
The draws below stay inside these ranges and needn't reach their ends.
Inputs may be any that keep to these rules, and one draw needn't show every extreme that they name: `expert_ids`: each token names 8 different experts: two from each of 4 different groups of 4 consecutive experts (group e // 4), one from each half of the group (e // 2). Among the 64 tokens of one index of node, two groups are named by exactly 40 tokens, four by exactly 32 and two by exactly 24.
All inputs are finite; a program needn't handle non-finite values.
Results may differ from the reference program's by a relative error of at most 0.012.
Values may be sent and summed in bfloat16 or wider, within the bound.
A program may use at most 192 MiB of HBM per device.

```python
import jax
import jax.numpy as jnp
import numpy as np
from jax import lax

D = 7168
HID = 2048
EXPERTS = 32
TOP = 8
TOK_NODE = 64
TOKENS = 512
CAP = 40
EXP_NODE = 4
HID_DEV = 512
N_NODE = 8
N_LOCAL = 4


def draw_expert_ids(key, part):
    key = jax.random.fold_in(key, 7)
    eighth = TOK_NODE // 8
    middle = TOK_NODE // 2
    counts = np.array([middle + eighth] * 2 + [middle] * 4 + [middle - eighth] * 2)
    bounds = np.cumsum(counts)
    slot_list = np.arange(4 * TOK_NODE)
    labels = np.searchsorted(bounds, slot_list, side='right')
    group_table = np.zeros((TOK_NODE, 4), dtype=np.int32)
    group_table[slot_list % TOK_NODE, slot_list // TOK_NODE] = labels
    fixed_table = jnp.asarray(group_table)

    def one_block(block_key):
        key_groups, key_order, key_halves = jax.random.split(block_key, 3)
        relabel = jax.random.permutation(key_groups, 8)
        row_order = jax.random.permutation(key_order, TOK_NODE)
        halves = jax.random.randint(key_halves, (TOK_NODE, 4, 2), 0, 2)
        groups = relabel[fixed_table][row_order]
        chosen = 4 * groups[:, :, None] + 2 * jnp.arange(2)[None, None, :] + halves
        return chosen.reshape(TOK_NODE, TOP)
    blocks = jax.random.split(key, TOKENS // TOK_NODE)
    return jax.vmap(one_block)(blocks).reshape(TOKENS, TOP).astype(jnp.int32)


def shard_levels(key, shape, shards, least, largest):
    level, own = 1.0, jax.random.fold_in(key, 6)
    for axis_at, shards_of in shards:
        steps = jnp.exp(jax.random.uniform(jax.random.fold_in(own, axis_at), (shards_of,), jnp.float32, least / len(shards), largest / len(shards)))
        level = level * jnp.repeat(steps, shape[axis_at] // shards_of).reshape([-1 if axis == axis_at else 1 for axis in range(len(shape))])
    return level


def normal_values(rng, extent, width, limit, pieces=(), held_as=jnp.bfloat16):
    result = jax.random.normal(rng, extent, jnp.float32) * width
    if len(pieces) > 0:
        result = shard_levels(rng, extent, pieces, -0.22, 0.18) * result
    return jnp.clip(result, min=-limit, max=limit).astype(held_as)


def setup_inputs(seed: int = 0) -> dict:
    streams_of = jax.random.split(jax.random.key(seed), 7)
    tokens = normal_values(streams_of[0], (TOKENS, D), 1.0, 6.0, ((0, 8),))
    router_weight = normal_values(streams_of[1], (D, EXPERTS), (D // 4) ** -0.5, 0.125)
    expert_ids = draw_expert_ids(jax.random.fold_in(streams_of[6], 71), 0)
    gate_weight = normal_values(streams_of[3], (EXPERTS, D, HID), D ** -0.5, 0.0625, ((0, 8), (2, 4)))
    up_weight = normal_values(streams_of[4], (EXPERTS, D, HID), D ** -0.5, 0.0625, ((0, 8), (2, 4)))
    down_weight = normal_values(streams_of[5], (EXPERTS, HID, D), HID ** -0.5, 0.125, ((0, 8), (1, 4)))
    return dict(tokens=tokens, router_weight=router_weight, expert_ids=expert_ids, gate_weight=gate_weight, up_weight=up_weight, down_weight=down_weight)


ROUTE_SCALE = 2.5


def reference(tokens, router_weight, expert_ids, gate_weight, up_weight, down_weight):
    scores = jax.nn.sigmoid(jnp.dot(tokens, router_weight, preferred_element_type=jnp.float32))
    picked = jnp.any(expert_ids[:, :, None] == jnp.arange(EXPERTS, dtype=jnp.int32)[None, None, :], axis=1)
    chosen_scores = jnp.where(picked, scores, 0.0)
    weights = (ROUTE_SCALE * chosen_scores / jnp.sum(chosen_scores, axis=1, keepdims=True)).astype(jnp.bfloat16)
    reached = jnp.any(picked.reshape(TOKENS, N_NODE, EXP_NODE), axis=2)
    rows_max = N_NODE * CAP

    def one_node(accumulated, node_index):
        token_index = jnp.nonzero(reached[:, node_index], size=rows_max, fill_value=0)[0].astype(jnp.int32)
        row_count = jnp.sum(reached[:, node_index].astype(jnp.int32))
        valid_rows = jnp.arange(rows_max, dtype=jnp.int32) < row_count
        node_rows = tokens[token_index].astype(jnp.float32)
        start = (node_index * EXP_NODE).astype(jnp.int32)
        node_gate = lax.dynamic_slice_in_dim(gate_weight, start, EXP_NODE, 0).astype(jnp.float32)
        node_up = lax.dynamic_slice_in_dim(up_weight, start, EXP_NODE, 0).astype(jnp.float32)
        node_down = lax.dynamic_slice_in_dim(down_weight, start, EXP_NODE, 0).astype(jnp.float32)
        node_weight = lax.dynamic_slice_in_dim(weights, start, EXP_NODE, 1)[token_index].astype(jnp.float32)
        gate_out = jnp.einsum('rd,edh->reh', node_rows, node_gate)
        up_out = jnp.einsum('rd,edh->reh', node_rows, node_up)
        hidden = (node_weight[:, :, None] * jax.nn.silu(gate_out) * up_out).astype(jnp.bfloat16)
        hidden = lax.optimization_barrier(hidden).astype(jnp.float32)
        hidden_split = hidden.reshape(rows_max, EXP_NODE, N_LOCAL, HID_DEV)
        down_split = node_down.reshape(EXP_NODE, N_LOCAL, HID_DEV, D)
        part = jnp.einsum('relh,elhd->rld', hidden_split, down_split).astype(jnp.bfloat16)
        part = lax.optimization_barrier(part).astype(jnp.float32)
        node_out = jnp.sum(part, axis=1).astype(jnp.bfloat16)
        node_out = lax.optimization_barrier(node_out).astype(jnp.float32)
        node_out = jnp.where(valid_rows[:, None], node_out, jnp.float32(0.0))
        return accumulated.at[token_index].add(node_out), None

    accumulated = jnp.zeros((TOKENS, D), jnp.float32)
    accumulated, unused = lax.scan(one_node, accumulated, jnp.arange(N_NODE, dtype=jnp.int32))
    return accumulated.astype(jnp.bfloat16)
```

```python
import functools

import jax
import jax.numpy as jnp
from jax import lax
from jax.experimental import pallas as pl
from jax.experimental.pallas import tpu as pltpu
from jax.sharding import PartitionSpec as P

EXPERTS = 32
CAP = 40
ROUTE_SCALE = 2.5
MESH = pl.DeviceIdType.MESH
LANES = 128
PARTS = 7
LAG = 2


def place(nodes, locals_):
    me, l = lax.axis_index("node"), lax.axis_index("local")
    return me, l, lax.div(me, 2), lax.rem(me, 2), lax.div(l, 2), lax.rem(l, 2)


def greet(nodes, ys):
    me, l, z, x, y, c = place(nodes, ys * 2)
    barrier = pltpu.get_barrier_semaphore()
    for k in range(1, nodes):
        pl.semaphore_signal(
            barrier, inc=1, device_id=(lax.rem(me + k, nodes), l), device_id_type=MESH
        )
    for dy in range(1, ys):
        pl.semaphore_signal(
            barrier, inc=1, device_id=(me, lax.rem(y + dy, ys) * 2 + c), device_id_type=MESH
        )
    pl.semaphore_signal(barrier, inc=1, device_id=(me, y * 2 + 1 - c), device_id_type=MESH)
    pl.semaphore_wait(barrier, nodes - 1 + ys)


def remote(src, dst, send_sem, recv_sem, device):
    return pltpu.make_async_remote_copy(
        src_ref=src, dst_ref=dst, send_sem=send_sem, recv_sem=recv_sem,
        device_id=device, device_id_type=MESH,
    )


def dispatch_kernel(
    nodes, ys, slots,
    send, sendw, gate, up, hid,
    recv, recvw, rows, acc, wbuf,
    wsem, n_ss, n_rs, w_ss, w_rs, y_ss, y_rs, c_ss, c_rs,
):
    me, l, z, x, y, c = place(nodes, ys * 2)
    zs = nodes // 2
    pair = 2 * CAP
    experts = gate.shape[0]
    share = send.shape[2]
    tiles = 2 * ys * experts
    sib = (me, y * 2 + 1 - c)

    def quarter(qi):
        dy, dc = lax.div(qi, 2), lax.rem(qi, 2)
        return lax.rem(y + ys - dy, ys) * 2 + lax.rem(c + dc, 2)

    def fetch(t, slot):
        q = quarter(lax.div(t, experts))
        e = lax.rem(t, experts)
        at = pl.ds(pl.multiple_of(q * share, LANES), share)
        return (
            pltpu.make_async_copy(gate.at[e, at, :], wbuf.at[slot, 0], wsem.at[slot, 0]),
            pltpu.make_async_copy(up.at[e, at, :], wbuf.at[slot, 1], wsem.at[slot, 1]),
        )

    for t in range(min(slots, tiles)):
        for copy in fetch(jnp.int32(t), t):
            copy.start()

    greet(nodes, ys)

    def node_copies(dz, dx):
        m = lax.rem(z + dz, zs) * 2 + lax.rem(x + dx, 2)
        k = dz * 2 + dx
        return (
            remote(send.at[m], recv.at[me], n_ss.at[k], n_rs.at[k], (m, l)),
            remote(sendw.at[m], recvw.at[me], w_ss.at[k], w_rs.at[k], (m, l)),
        )

    def block(q, dz):
        zz = lax.rem(z + zs - dz, zs)
        return rows.at[q, pl.ds(pl.multiple_of(zz * pair, 16), pair), :]

    def y_copy(dz, dy):
        return remote(
            block(l, dz), block(l, dz), y_ss.at[dz, dy], y_rs.at[dz, dy],
            (me, lax.rem(y + dy, ys) * 2 + c),
        )

    def sib_copy(dz, dy):
        q = lax.rem(y + ys - dy, ys) * 2 + c
        return remote(block(q, dz), block(q, dz), c_ss.at[dz, dy], c_rs.at[dz, dy], sib)

    for dz in range(zs):
        for dx in range(2):
            if dz + dx > 0:
                for copy in node_copies(dz, dx):
                    copy.start()
    recv[me] = send[me]
    recvw[me] = sendw[me]

    def forward(dz):
        for dy in range(1, ys):
            y_copy(dz, dy).wait_recv()
            sib_copy(dz, dy).start()

    for dz in range(zs):
        for dx in range(2):
            if dz + dx > 0:
                for copy in node_copies(dz, dx):
                    copy.wait_recv()
        zz = lax.rem(z + zs - dz, zs)
        got = recv[pl.ds(zz * 2, 2)].astype(jnp.float32).reshape(pair, share)
        rows[l, pl.ds(pl.multiple_of(zz * pair, 16), pair), :] = got.astype(jnp.bfloat16)
        for dy in range(1, ys):
            y_copy(dz, dy).start()
        sib_copy(dz, 0).start()
        if dz > 0:
            forward(dz - 1)

    for qi in range(2 * ys):
        dy, dc = qi // 2, qi % 2
        if qi == 1:
            forward(zs - 1)
        if dc == 1:
            for dz in range(zs):
                sib_copy(dz, dy).wait_recv()
        q = quarter(jnp.int32(qi))

        def step(e, carry):
            t = qi * experts + e
            slot = lax.rem(t, slots)
            for copy in fetch(t, slot):
                copy.wait()
            for g in range(2):
                part = jnp.dot(rows[q], wbuf[slot, g], preferred_element_type=jnp.float32)
                if qi == 0:
                    acc[e, g] = part
                else:
                    acc[e, g] += part

            @pl.when(t + slots < tiles)
            def _():
                for copy in fetch(t + slots, slot):
                    copy.start()

            return carry

        lax.fori_loop(0, experts, step, 0)

    gain = recvw[...].astype(jnp.float32).reshape(nodes * CAP, LANES)
    width = gate.shape[2]
    for e in range(experts):
        v = acc[e, 0]
        value = gain[:, e:e + 1] * (v / (1.0 + jnp.exp(-v))) * acc[e, 1]
        hid[:, e * width:(e + 1) * width] = value.astype(jnp.bfloat16)

    for dz in range(zs):
        for dx in range(2):
            if dz + dx > 0:
                for copy in node_copies(dz, dx):
                    copy.wait_send()
        for dy in range(ys):
            if dy > 0:
                y_copy(dz, dy).wait_send()
            sib_copy(dz, dy).wait_send()


def combine_kernel(
    nodes, ys,
    hid, down, back, out,
    wbuf, own, psib, gsib, psum, gsum, pnode, gnode,
    wsem, c_ss, c_rs, y_ss, y_rs, n_ss, n_rs,
):
    me, l, z, x, y, c = place(nodes, ys * 2)
    share = out.shape[1]
    width = share // PARTS
    sib = (me, y * 2 + 1 - c)

    def fetch(f, d, dc):
        q = lax.rem(y + d + 1, ys) * 2 + lax.rem(c + dc, 2)
        at = pl.ds(pl.multiple_of(q * share + f * width, LANES), width)
        return pltpu.make_async_copy(down.at[:, at], wbuf.at[f, d, dc], wsem.at[f, d, dc])

    def start_weights(f, carry):
        for d in range(ys):
            for dc in (1, 0):
                fetch(f, d, dc).start()
        return carry

    lax.fori_loop(0, PARTS, start_weights, 0)
    greet(nodes, ys)

    def sib_copy(f, d):
        return remote(psib.at[f, d], gsib.at[f, d], c_ss.at[f, d], c_rs.at[f, d], sib)

    def y_copy(f, d):
        to = (me, lax.rem(y + d + 1, ys) * 2 + c)
        return remote(psum.at[f, d], gsum.at[f, d], y_ss.at[f, d], y_rs.at[f, d], to)

    def node_copy(f, k):
        m = lax.rem(me + k, nodes)
        return remote(pnode.at[f, m], gnode.at[f, me], n_ss.at[f, k], n_rs.at[f, k], (m, l))

    def step(f, carry):
        @pl.when(f < PARTS)
        def _():
            for d in range(ys):
                fetch(f, d, 1).wait()
                part = jnp.dot(hid[...], wbuf[f, d, 1], preferred_element_type=jnp.float32)
                psib[f, d] = part.astype(jnp.bfloat16)
                sib_copy(f, d).start()
                fetch(f, d, 0).wait()
                own[f, d] = jnp.dot(hid[...], wbuf[f, d, 0], preferred_element_type=jnp.float32)
            for d in range(ys - 1):
                sib_copy(f, d).wait_recv()
                psum[f, d] = (own[f, d] + gsib[f, d].astype(jnp.float32)).astype(jnp.bfloat16)
                y_copy(f, d).start()

        @pl.when(f >= LAG)
        def _():
            g = f - LAG
            sib_copy(g, ys - 1).wait_recv()
            total = own[g, ys - 1] + gsib[g, ys - 1].astype(jnp.float32)
            for d in range(ys - 1):
                y_copy(g, d).wait_recv()
                total += gsum[g, d].astype(jnp.float32)
            pnode[g] = total.reshape(nodes, CAP, width).astype(jnp.bfloat16)
            for k in range(1, nodes):
                node_copy(g, k).start()
            gnode[g, me] = pnode[g, me]

        return carry

    lax.fori_loop(0, PARTS + LAG, step, 0)

    def finish(f, carry):
        for k in range(1, nodes):
            node_copy(f, k).wait_recv()
        got = gnode[f].astype(jnp.float32).reshape(nodes * CAP, width).astype(jnp.bfloat16)
        at = pl.ds(pl.multiple_of(f * width, LANES), width)
        out[:, at] = jnp.dot(back[...], got, preferred_element_type=jnp.float32).astype(jnp.bfloat16)
        return carry

    lax.fori_loop(0, PARTS, finish, 0)

    def drain(f, carry):
        for d in range(ys):
            sib_copy(f, d).wait_send()
            if d < ys - 1:
                y_copy(f, d).wait_send()
        for k in range(1, nodes):
            node_copy(f, k).wait_send()
        return carry

    lax.fori_loop(0, PARTS, drain, 0)


def body(tokens, router_weight, expert_ids, gate_weight, up_weight, down_weight):
    nodes = lax.axis_size("node")
    locals_ = lax.axis_size("local")
    ys, zs = locals_ // 2, nodes // 2
    experts, dim, hid_dev = gate_weight.shape
    rows_dev = tokens.shape[0]
    share = dim // locals_
    total_rows = nodes * CAP
    bf16, f32 = jnp.bfloat16, jnp.float32
    scores = jax.nn.sigmoid(jnp.dot(tokens, router_weight, preferred_element_type=f32))
    picked = jnp.any(
        expert_ids[:, :, None] == jnp.arange(EXPERTS, dtype=jnp.int32)[None, None, :], axis=1
    )
    chosen = jnp.where(picked, scores, 0.0)
    weights = (ROUTE_SCALE * chosen / jnp.sum(chosen, axis=1, keepdims=True)).astype(bf16)
    node_weights = weights.reshape(rows_dev, nodes, experts)
    reached = jnp.any(picked.reshape(rows_dev, nodes, experts), axis=2)
    slot_index = jnp.cumsum(reached.astype(jnp.int32), axis=0) - 1
    positions = jnp.arange(CAP, dtype=jnp.int32)[None, :, None]
    onehot = (reached.T[:, None, :] & (slot_index.T[:, None, :] == positions)).astype(bf16)
    send_w = jnp.einsum(
        "mct,tme->mce", onehot, node_weights, preferred_element_type=f32
    ).astype(bf16)
    send_w = jnp.pad(send_w, ((0, 0), (0, 0), (0, LANES - experts)))
    mine = lax.dynamic_slice_in_dim(tokens, lax.axis_index("local") * share, share, 1)
    send = jnp.einsum("mct,td->mcd", onehot, mine, preferred_element_type=f32).astype(bf16)
    back = onehot.transpose(2, 0, 1).reshape(rows_dev, total_rows)

    vmem = pl.BlockSpec(memory_space=pltpu.VMEM)
    hbm = pl.BlockSpec(memory_space=pl.ANY)
    dma = pltpu.SemaphoreType.DMA
    tiles = locals_ * experts
    slots = min(tiles, 10)
    hidden = pl.pallas_call(
        functools.partial(dispatch_kernel, nodes, ys, slots),
        out_shape=jax.ShapeDtypeStruct((total_rows, experts * hid_dev), bf16),
        in_specs=[vmem, vmem, hbm, hbm],
        out_specs=vmem,
        scratch_shapes=[
            pltpu.VMEM((nodes, CAP, share), bf16),
            pltpu.VMEM((nodes, CAP, LANES), bf16),
            pltpu.VMEM((locals_, total_rows, share), bf16),
            pltpu.VMEM((experts, 2, total_rows, hid_dev), f32),
            pltpu.VMEM((slots, 2, share, hid_dev), bf16),
            dma((slots, 2)),
            dma((nodes,)), dma((nodes,)), dma((nodes,)), dma((nodes,)),
            dma((zs, ys)), dma((zs, ys)), dma((zs, ys)), dma((zs, ys)),
        ],
        compiler_params=pltpu.CompilerParams(
            collective_id=0, has_side_effects=True, vmem_limit_bytes=58 * 2**20
        ),
        cost_estimate=pl.CostEstimate(
            flops=4 * total_rows * dim * experts * hid_dev,
            bytes_accessed=4 * experts * dim * hid_dev,
            transcendentals=total_rows * experts * hid_dev,
        ),
    )(send, send_w, gate_weight, up_weight)

    width = share // PARTS
    return pl.pallas_call(
        functools.partial(combine_kernel, nodes, ys),
        out_shape=jax.ShapeDtypeStruct((rows_dev, share), bf16),
        in_specs=[vmem, hbm, vmem],
        out_specs=vmem,
        scratch_shapes=[
            pltpu.VMEM((PARTS, ys, 2, experts * hid_dev, width), bf16),
            pltpu.VMEM((PARTS, ys, total_rows, width), f32),
            pltpu.VMEM((PARTS, ys, total_rows, width), bf16),
            pltpu.VMEM((PARTS, ys, total_rows, width), bf16),
            pltpu.VMEM((PARTS, ys - 1, total_rows, width), bf16),
            pltpu.VMEM((PARTS, ys - 1, total_rows, width), bf16),
            pltpu.VMEM((PARTS, nodes, CAP, width), bf16),
            pltpu.VMEM((PARTS, nodes, CAP, width), bf16),
            dma((PARTS, ys, 2)),
            dma((PARTS, ys)), dma((PARTS, ys)),
            dma((PARTS, ys)), dma((PARTS, ys)),
            dma((PARTS, nodes)), dma((PARTS, nodes)),
        ],
        compiler_params=pltpu.CompilerParams(
            collective_id=1, has_side_effects=True, vmem_limit_bytes=58 * 2**20
        ),
        cost_estimate=pl.CostEstimate(
            flops=2 * total_rows * dim * experts * hid_dev,
            bytes_accessed=2 * experts * dim * hid_dev,
            transcendentals=0,
        ),
    )(hidden, down_weight.reshape(experts * hid_dev, dim), back)


def solution(mesh):
    return jax.shard_map(
        body,
        mesh=mesh,
        in_specs=(
            P("node", None),
            P(),
            P("node", None),
            P("node", None, "local"),
            P("node", None, "local"),
            P("node", "local", None),
        ),
        out_specs=P("node", "local"),
        check_vma=False,
    )
```

```python
import functools

import jax
import jax.numpy as jnp
from jax import lax
from jax.experimental import pallas as pl
from jax.experimental.pallas import tpu as pltpu
from jax.sharding import PartitionSpec as P

EXPERTS = 32
CAP = 40
ROUTE_SCALE = 2.5
MESH = pl.DeviceIdType.MESH
LANES = 128
PARTS = 7
WINDOW = 3
LAG = 2


def place(nodes, locals_):
    me, l = lax.axis_index("node"), lax.axis_index("local")
    return me, l, lax.div(me, 2), lax.rem(me, 2), lax.div(l, 2), lax.rem(l, 2)


def greet(nodes, ys):
    me, l, z, x, y, c = place(nodes, ys * 2)
    barrier = pltpu.get_barrier_semaphore()
    for k in range(1, nodes):
        pl.semaphore_signal(
            barrier, inc=1, device_id=(lax.rem(me + k, nodes), l), device_id_type=MESH
        )
    for dy in range(1, ys):
        pl.semaphore_signal(
            barrier, inc=1, device_id=(me, lax.rem(y + dy, ys) * 2 + c), device_id_type=MESH
        )
    pl.semaphore_signal(barrier, inc=1, device_id=(me, y * 2 + 1 - c), device_id_type=MESH)
    pl.semaphore_wait(barrier, nodes - 1 + ys)


def remote(src, dst, send_sem, recv_sem, device):
    return pltpu.make_async_remote_copy(
        src_ref=src, dst_ref=dst, send_sem=send_sem, recv_sem=recv_sem,
        device_id=device, device_id_type=MESH,
    )


def dispatch_kernel(
    nodes, ys, slots,
    send, sendw, gate, up, hid,
    recv, recvw, rows, acc, wbuf,
    wsem, n_ss, n_rs, w_ss, w_rs, y_ss, y_rs, c_ss, c_rs,
):
    me, l, z, x, y, c = place(nodes, ys * 2)
    total = nodes * CAP
    experts, locals_, _, width, units = gate.shape
    tiles = PARTS * experts
    sib = (me, y * 2 + 1 - c)

    def fetch(t, slot):
        h, e = lax.div(t, experts), lax.rem(t, experts)
        return (
            pltpu.make_async_copy(
                gate.at[e, :, h], wbuf.at[slot, :, :, :units], wsem.at[slot, 0]
            ),
            pltpu.make_async_copy(
                up.at[e, :, h], wbuf.at[slot, :, :, units:], wsem.at[slot, 1]
            ),
        )

    def first(t, carry):
        for copy in fetch(t, t):
            copy.start()
        return carry

    lax.fori_loop(0, slots, first, 0)
    greet(nodes, ys)

    def node_copy(h, k):
        m = lax.rem(me + k, nodes)
        at = pl.ds(pl.multiple_of(h * width, LANES), width)
        return remote(
            send.at[m, :, at], recv.at[h, me], n_ss.at[h, k], n_rs.at[h, k], (m, l)
        )

    def gain_copy(k):
        m = lax.rem(me + k, nodes)
        return remote(sendw.at[m], recvw.at[me], w_ss.at[k], w_rs.at[k], (m, l))

    def block(h, q):
        return rows.at[h, :, pl.ds(pl.multiple_of(q * width, LANES), width)]

    def y_copy(h, dy):
        to = (me, lax.rem(y + dy, ys) * 2 + c)
        return remote(block(h, l), block(h, l), y_ss.at[h, dy], y_rs.at[h, dy], to)

    def sib_copy(h, dy):
        q = lax.rem(y + ys - dy, ys) * 2 + c
        return remote(block(h, q), block(h, q), c_ss.at[h, dy], c_rs.at[h, dy], sib)

    def send_all(h, carry):
        for k in range(1, nodes):
            node_copy(h, k).start()
        at = pl.ds(pl.multiple_of(h * width, LANES), width)
        recv[h, me] = send[me, :, at]
        return carry

    lax.fori_loop(0, WINDOW, send_all, 0)
    for k in range(1, nodes):
        gain_copy(k).start()
    recvw[me] = sendw[me]
    acc[...] = jnp.zeros(acc.shape, jnp.float32)

    def step(i, carry):
        @pl.when(i < PARTS)
        def _():
            for k in range(1, nodes):
                node_copy(i, k).wait_recv()
            got = recv[i].astype(jnp.float32).reshape(total, width)
            at = pl.ds(pl.multiple_of(l * width, LANES), width)
            rows[i, :, at] = got.astype(jnp.bfloat16)
            for dy in range(1, ys):
                y_copy(i, dy).start()
            sib_copy(i, 0).start()

            @pl.when(i + WINDOW < PARTS)
            def _():
                send_all(i + WINDOW, 0)

        @pl.when((i >= 1) & (i <= PARTS))
        def _():
            for dy in range(1, ys):
                y_copy(i - 1, dy).wait_recv()
                sib_copy(i - 1, dy).start()

        @pl.when(i >= 2)
        def _():
            h = i - 2
            for dy in range(ys):
                sib_copy(h, dy).wait_recv()

            def expert(e, carry):
                t = h * experts + e
                slot = lax.rem(t, slots)
                for copy in fetch(t, slot):
                    copy.wait()
                acc[e] += jnp.dot(
                    rows[h], wbuf[slot].reshape(locals_ * width, 2 * units),
                    preferred_element_type=jnp.float32,
                )

                @pl.when(t + slots < tiles)
                def _():
                    for copy in fetch(t + slots, slot):
                        copy.start()

                return carry

            lax.fori_loop(0, experts, expert, 0)

        return carry

    lax.fori_loop(0, PARTS + 2, step, 0)

    for k in range(1, nodes):
        gain_copy(k).wait_recv()
    gain = recvw[...].astype(jnp.float32).reshape(total, LANES)
    for e in range(experts):
        v = acc[e, :, :units]
        value = gain[:, e:e + 1] * (v / (1.0 + jnp.exp(-v))) * acc[e, :, units:]
        hid[:, e * units:(e + 1) * units] = value.astype(jnp.bfloat16)

    def drain(h, carry):
        for k in range(1, nodes):
            node_copy(h, k).wait_send()
        for dy in range(ys):
            if dy > 0:
                y_copy(h, dy).wait_send()
            sib_copy(h, dy).wait_send()
        return carry

    lax.fori_loop(0, PARTS, drain, 0)
    for k in range(1, nodes):
        gain_copy(k).wait_send()


def combine_kernel(
    nodes, ys,
    hid, down, back, out,
    wbuf, own, psib, gsib, psum, gsum, pnode, gnode,
    wsem, c_ss, c_rs, y_ss, y_rs, n_ss, n_rs,
):
    me, l, z, x, y, c = place(nodes, ys * 2)
    share = out.shape[1]
    width = share // PARTS
    sib = (me, y * 2 + 1 - c)

    def fetch(f, d, dc):
        q = lax.rem(y + d + 1, ys) * 2 + lax.rem(c + dc, 2)
        at = pl.ds(pl.multiple_of(q * share + f * width, LANES), width)
        half = wbuf.at[f, d, :, (1 - dc) * width:(2 - dc) * width]
        return pltpu.make_async_copy(down.at[:, at], half, wsem.at[f, d, dc])

    def start_weights(f, carry):
        for d in range(ys):
            for dc in (1, 0):
                fetch(f, d, dc).start()
        return carry

    lax.fori_loop(0, PARTS, start_weights, 0)
    greet(nodes, ys)

    def sib_copy(f, d):
        return remote(psib.at[f, d], gsib.at[f, d], c_ss.at[f, d], c_rs.at[f, d], sib)

    def y_copy(f, d):
        to = (me, lax.rem(y + d + 1, ys) * 2 + c)
        return remote(psum.at[f, d], gsum.at[f, d], y_ss.at[f, d], y_rs.at[f, d], to)

    def node_copy(f, k):
        m = lax.rem(me + k, nodes)
        return remote(pnode.at[f, m], gnode.at[f, me], n_ss.at[f, k], n_rs.at[f, k], (m, l))

    def step(f, carry):
        @pl.when(f < PARTS)
        def _():
            for d in range(ys):
                fetch(f, d, 1).wait()
                fetch(f, d, 0).wait()
                part = jnp.dot(hid[...], wbuf[f, d], preferred_element_type=jnp.float32)
                psib[f, d] = part[:, :width].astype(jnp.bfloat16)
                sib_copy(f, d).start()
                own[f, d] = part[:, width:]
            for d in range(ys - 1):
                sib_copy(f, d).wait_recv()
                psum[f, d] = (own[f, d] + gsib[f, d].astype(jnp.float32)).astype(jnp.bfloat16)
                y_copy(f, d).start()

        @pl.when(f >= LAG)
        def _():
            g = f - LAG
            sib_copy(g, ys - 1).wait_recv()
            total = own[g, ys - 1] + gsib[g, ys - 1].astype(jnp.float32)
            for d in range(ys - 1):
                y_copy(g, d).wait_recv()
                total += gsum[g, d].astype(jnp.float32)
            pnode[g] = total.reshape(nodes, CAP, width).astype(jnp.bfloat16)
            for k in range(1, nodes):
                node_copy(g, k).start()
            gnode[g, me] = pnode[g, me]

        return carry

    lax.fori_loop(0, PARTS + LAG, step, 0)

    def finish(f, carry):
        for k in range(1, nodes):
            node_copy(f, k).wait_recv()
        got = gnode[f].astype(jnp.float32).reshape(nodes * CAP, width).astype(jnp.bfloat16)
        at = pl.ds(pl.multiple_of(f * width, LANES), width)
        out[:, at] = jnp.dot(back[...], got, preferred_element_type=jnp.float32).astype(jnp.bfloat16)
        return carry

    lax.fori_loop(0, PARTS, finish, 0)

    def drain(f, carry):
        for d in range(ys):
            sib_copy(f, d).wait_send()
            if d < ys - 1:
                y_copy(f, d).wait_send()
        for k in range(1, nodes):
            node_copy(f, k).wait_send()
        return carry

    lax.fori_loop(0, PARTS, drain, 0)


def body(tokens, router_weight, expert_ids, gate_weight, up_weight, down_weight):
    nodes = lax.axis_size("node")
    locals_ = lax.axis_size("local")
    ys = locals_ // 2
    experts, dim, hid_dev = gate_weight.shape
    rows_dev = tokens.shape[0]
    share = dim // locals_
    total_rows = nodes * CAP
    bf16, f32 = jnp.bfloat16, jnp.float32
    scores = jax.nn.sigmoid(jnp.dot(tokens, router_weight, preferred_element_type=f32))
    picked = jnp.any(
        expert_ids[:, :, None] == jnp.arange(EXPERTS, dtype=jnp.int32)[None, None, :], axis=1
    )
    chosen = jnp.where(picked, scores, 0.0)
    weights = (ROUTE_SCALE * chosen / jnp.sum(chosen, axis=1, keepdims=True)).astype(bf16)
    node_weights = weights.reshape(rows_dev, nodes, experts)
    reached = jnp.any(picked.reshape(rows_dev, nodes, experts), axis=2)
    slot_index = jnp.cumsum(reached.astype(jnp.int32), axis=0) - 1
    positions = jnp.arange(CAP, dtype=jnp.int32)[None, :, None]
    onehot = (reached.T[:, None, :] & (slot_index.T[:, None, :] == positions)).astype(bf16)
    send_w = jnp.einsum(
        "mct,tme->mce", onehot, node_weights, preferred_element_type=f32
    ).astype(bf16)
    send_w = jnp.pad(send_w, ((0, 0), (0, 0), (0, LANES - experts)))
    mine = lax.dynamic_slice_in_dim(tokens, lax.axis_index("local") * share, share, 1)
    send = jnp.einsum("mct,td->mcd", onehot, mine, preferred_element_type=f32).astype(bf16)
    back = onehot.transpose(2, 0, 1).reshape(rows_dev, total_rows)

    vmem = pl.BlockSpec(memory_space=pltpu.VMEM)
    hbm = pl.BlockSpec(memory_space=pl.ANY)
    dma = pltpu.SemaphoreType.DMA
    width = share // PARTS
    slots = min(PARTS * experts, 18)
    pieces = (experts, locals_, PARTS, width, hid_dev)
    hidden = pl.pallas_call(
        functools.partial(dispatch_kernel, nodes, ys, slots),
        out_shape=jax.ShapeDtypeStruct((total_rows, experts * hid_dev), bf16),
        in_specs=[vmem, vmem, hbm, hbm],
        out_specs=vmem,
        scratch_shapes=[
            pltpu.VMEM((PARTS, nodes, CAP, width), bf16),
            pltpu.VMEM((nodes, CAP, LANES), bf16),
            pltpu.VMEM((PARTS, total_rows, locals_ * width), bf16),
            pltpu.VMEM((experts, total_rows, 2 * hid_dev), f32),
            pltpu.VMEM((slots, locals_, width, 2 * hid_dev), bf16),
            dma((slots, 2)),
            dma((PARTS, nodes)), dma((PARTS, nodes)), dma((nodes,)), dma((nodes,)),
            dma((PARTS, ys)), dma((PARTS, ys)), dma((PARTS, ys)), dma((PARTS, ys)),
        ],
        compiler_params=pltpu.CompilerParams(
            collective_id=0, has_side_effects=True, vmem_limit_bytes=58 * 2**20
        ),
        cost_estimate=pl.CostEstimate(
            flops=4 * total_rows * dim * experts * hid_dev,
            bytes_accessed=4 * experts * dim * hid_dev,
            transcendentals=total_rows * experts * hid_dev,
        ),
    )(send, send_w, gate_weight.reshape(pieces), up_weight.reshape(pieces))

    return pl.pallas_call(
        functools.partial(combine_kernel, nodes, ys),
        out_shape=jax.ShapeDtypeStruct((rows_dev, share), bf16),
        in_specs=[vmem, hbm, vmem],
        out_specs=vmem,
        scratch_shapes=[
            pltpu.VMEM((PARTS, ys, experts * hid_dev, 2 * width), bf16),
            pltpu.VMEM((PARTS, ys, total_rows, width), f32),
            pltpu.VMEM((PARTS, ys, total_rows, width), bf16),
            pltpu.VMEM((PARTS, ys, total_rows, width), bf16),
            pltpu.VMEM((PARTS, ys - 1, total_rows, width), bf16),
            pltpu.VMEM((PARTS, ys - 1, total_rows, width), bf16),
            pltpu.VMEM((PARTS, nodes, CAP, width), bf16),
            pltpu.VMEM((PARTS, nodes, CAP, width), bf16),
            dma((PARTS, ys, 2)),
            dma((PARTS, ys)), dma((PARTS, ys)),
            dma((PARTS, ys)), dma((PARTS, ys)),
            dma((PARTS, nodes)), dma((PARTS, nodes)),
        ],
        compiler_params=pltpu.CompilerParams(
            collective_id=1, has_side_effects=True, vmem_limit_bytes=58 * 2**20
        ),
        cost_estimate=pl.CostEstimate(
            flops=2 * total_rows * dim * experts * hid_dev,
            bytes_accessed=2 * experts * dim * hid_dev,
            transcendentals=0,
        ),
    )(hidden, down_weight.reshape(experts * hid_dev, dim), back)


def solution(mesh):
    return jax.shard_map(
        body,
        mesh=mesh,
        in_specs=(
            P("node", None),
            P(),
            P("node", None),
            P("node", None, "local"),
            P("node", None, "local"),
            P("node", "local", None),
        ),
        out_specs=P("node", "local"),
        check_vma=False,
    )
```
